32 devices in a mesh: orbit: 8 (over z, y), region: 4 (over x, core).
Axes of the slice: x: 2, y: 2, z: 4, core: 2. Of those that a mesh axis runs over, the one named last changes fastest.
Arguments:
- footprints: bfloat16 [10240, 64, 256], P(('orbit', 'region')), may hold values from -0.0625 to 0.0625
- block_sounding: int32 [10240], P(('orbit', 'region')), may hold values from 0 to 31
- block_tile: int32 [10240], P(('orbit', 'region')), may hold values from 0 to 7
- block_count: int32 [32], P(('orbit', 'region')), may hold values from 80 to 320, as said below
- observations: float32 [256, 64, 128], P('orbit'), may hold values from -6 to 6
- obs_weight: float32 [256, 64], P('orbit'), may hold values from 0.25 to 4
- prior_std: float32 [4, 8, 256], P('region', 'orbit'), may hold values from 0.4 to 4.8
Outputs:
- flux: float32 [4, 8, 256, 128], P('region', 'orbit')
- residual: float32 [4, 8, 256, 128], P('region', 'orbit')
The draws below stay inside these ranges and needn't reach their ends.
Inputs may be any that keep to these rules, and one draw needn't show every extreme that they name: `block_sounding`: index of a sounding block among the 32 of the block's orbit index. `block_tile`: index of a tile among the 8 of the block's region; some tiles are named far more often than others. `block_count`: slots from this count on are unused; some device has all 320 slots live.
All inputs are finite; a program needn't handle non-finite values.
Results may differ from the reference program's by a relative error of at most 0.0068.
Values may be sent and summed in bfloat16 or wider, within the bound.
No kernel may reach another device: no remote copies, remote signals or barrier semaphores. Data moves between devices by JAX's collectives and lax.ppermute only.
A program may use at most 128 MiB of HBM per device.

```python
import math
import jax
import jax.numpy as jnp
import numpy as np
from jax import lax

SBLK = 64
CELLS = 256
NRHS = 128
ITERS = 2
NB = 320
SB_DEV = 32
BLOCKS = 10240
SBLOCKS = 256
TILES_REG = 8
N_ORBIT = 8
N_REGION = 4


def draw_block_count(key, part):
    first_key, second_key = jax.random.split(key)
    devices_all = N_ORBIT * N_REGION
    counts = jax.random.randint(first_key, (devices_all,), NB // 4, NB + 1)
    chosen = jax.random.randint(second_key, (), 0, devices_all)
    return jnp.where(jnp.arange(devices_all) == chosen, NB, counts).astype(jnp.int32)


def draw_prior_std(key, part):
    base = jax.random.uniform(key, (N_REGION, TILES_REG, CELLS), jnp.float32)
    rough = jnp.exp(jnp.log(0.4) + base * jnp.log(4.0))
    place = jnp.arange(N_REGION, dtype=jnp.float32)[:, None] * TILES_REG + jnp.arange(TILES_REG, dtype=jnp.float32)[None, :]
    ramp = 1.0 + 2.0 * place / (N_REGION * TILES_REG - 1)
    return (rough * ramp[:, :, None]).astype(jnp.float32)


def place_ends(entries, stream_key, least, largest):
    spot = [jax.random.randint(jax.random.fold_in(stream_key, axis), (), 0, length) for axis, length in enumerate(entries.shape)]
    longest = entries.shape.index(max(entries.shape))
    beside = spot[:longest] + [(spot[longest] + 1) % entries.shape[longest]] + spot[longest + 1:]
    return entries.at[tuple(spot)].set(least).at[tuple(beside)].set(largest)


def level_of(key, shape, cuts, least, top_value):
    factor_of, own = 1.0, jax.random.fold_in(key, 6)
    for position, shards_of in cuts:
        heights = jnp.exp(jax.random.uniform(jax.random.fold_in(own, position), (shards_of,), jnp.float32, least / len(cuts), top_value / len(cuts)))
        factor_of = factor_of * jnp.repeat(heights, shape[position] // shards_of).reshape([-1 if axis == position else 1 for axis in range(len(shape))])
    return factor_of


def cumulative_ranks(count, lean):
    weights = [(1 << 20) // math.isqrt(rank ** lean) + 1 for rank in range(1, count + 1)]
    scale = 1 + sum(weights) // (1 << 30)
    return np.cumsum(np.array([max(1, weight // scale) for weight in weights]))


def ranked_ids(stream_key, dims, number_of, skew):
    table = cumulative_ranks(number_of, skew)
    pick = jax.random.randint(jax.random.fold_in(stream_key, 1), dims, 0, int(table[number_of - 1]))
    standing = jnp.searchsorted(jnp.asarray(table, jnp.int32), pick, side="right")
    return jax.random.permutation(jax.random.fold_in(stream_key, 2), number_of)[standing].astype(jnp.int32)


def noise(rng, shape, spread, limit, cuts=(), held_as=jnp.bfloat16):
    level = level_of(rng, shape, cuts, -0.22, 0.18) if cuts else 1.0
    array = jax.random.normal(rng, shape, jnp.float32) * spread * level
    return jnp.minimum(jnp.maximum(array, -limit), limit).astype(held_as)


def setup_inputs(seed: int = 0) -> dict:
    streams_of = jax.random.split(jax.random.key(seed), 8)
    footprints = noise(streams_of[0], (BLOCKS, SBLK, CELLS), (CELLS * NB * N_REGION // SB_DEV) ** -0.5, 0.0625, ((0, 32),))
    block_sounding = place_ends(jax.random.randint(streams_of[1], (BLOCKS,), 0, SB_DEV), jax.random.fold_in(streams_of[1], 1), 0, SB_DEV - 1).astype(jnp.int32)
    block_tile = place_ends(ranked_ids(streams_of[2], (BLOCKS,), TILES_REG, 2), jax.random.fold_in(streams_of[2], 3), 0, TILES_REG - 1).astype(jnp.int32)
    block_count = draw_block_count(jax.random.fold_in(streams_of[7], 71), 0)
    observations = noise(streams_of[4], (SBLOCKS, SBLK, NRHS), 1.0, 6.0, ((0, 8),), jnp.float32)
    obs_weight = jnp.clip(jnp.exp(math.log(4.0) - 2.7725887 * jax.random.uniform(streams_of[5], (SBLOCKS, SBLK), jnp.float32) ** level_of(streams_of[5], (SBLOCKS, SBLK), ((0, 8),), -0.2, 0.2)), 0.25, 4.0)
    prior_std = draw_prior_std(jax.random.fold_in(streams_of[7], 71), 0)
    return dict(footprints=footprints, block_sounding=block_sounding, block_tile=block_tile, block_count=block_count, observations=observations, obs_weight=obs_weight, prior_std=prior_std)


def forward_map(footprints, block_sounding, block_tile, block_count, values):
    blocks = footprints.reshape(N_ORBIT * N_REGION, NB, SBLK, CELLS)
    sounds = block_sounding.reshape(N_ORBIT * N_REGION, NB)
    tile_ids = block_tile.reshape(N_ORBIT * N_REGION, NB)
    devices = jnp.arange(N_ORBIT * N_REGION, dtype=jnp.int32)

    def per_device(running, bundle):
        blocks_now, sound_ids, tile_now, live_count, device = bundle
        alive = (jnp.arange(NB) < live_count).astype(jnp.float32)
        region_values = lax.dynamic_index_in_dim(values, device % N_REGION, 0, keepdims=False)
        picked = region_values[tile_now].astype(jnp.float32)
        products = jnp.einsum("bsc,bcr->bsr", blocks_now.astype(jnp.float32), picked) * alive[:, None, None]
        local_sum = jax.ops.segment_sum(products, sound_ids, num_segments=SB_DEV)
        return running.at[device // N_REGION].add(local_sum), None

    start_sum = jnp.zeros((N_ORBIT, SB_DEV, SBLK, NRHS), jnp.float32)
    running, _ = lax.scan(per_device, start_sum, (blocks, sounds, tile_ids, block_count, devices))
    return running


def transpose_map(footprints, block_sounding, block_tile, block_count, weighted):
    blocks = footprints.reshape(N_ORBIT * N_REGION, NB, SBLK, CELLS)
    sounds = block_sounding.reshape(N_ORBIT * N_REGION, NB)
    tile_ids = block_tile.reshape(N_ORBIT * N_REGION, NB)
    devices = jnp.arange(N_ORBIT * N_REGION, dtype=jnp.int32)

    def per_device(running, bundle):
        blocks_now, sound_ids, tile_now, live_count, device = bundle
        alive = (jnp.arange(NB) < live_count).astype(jnp.float32)
        orbit_rows = lax.dynamic_index_in_dim(weighted, device // N_REGION, 0, keepdims=False)
        picked = orbit_rows[sound_ids].astype(jnp.float32)
        contrib = jnp.einsum("bsc,bsr->bcr", blocks_now.astype(jnp.float32), picked) * alive[:, None, None]
        local_sum = jax.ops.segment_sum(contrib, tile_now, num_segments=TILES_REG)
        return running.at[device % N_REGION].add(local_sum), None

    start_sum = jnp.zeros((N_REGION, TILES_REG, CELLS, NRHS), jnp.float32)
    running, _ = lax.scan(per_device, start_sum, (blocks, sounds, tile_ids, block_count, devices))
    return running


def reference(footprints, block_sounding, block_tile, block_count, observations, obs_weight, prior_std):
    weight = obs_weight.reshape(N_ORBIT, SB_DEV, SBLK, 1)
    observed = observations.reshape(N_ORBIT, SB_DEV, SBLK, NRHS)
    prior_scale = prior_std[..., None]
    weighted0 = lax.optimization_barrier((weight * observed).astype(jnp.bfloat16))
    right_side = prior_scale * transpose_map(footprints, block_sounding, block_tile, block_count, weighted0)
    iterate = jnp.zeros_like(right_side)
    residual = right_side
    direction = right_side
    norm_now = jnp.sum(residual * residual, axis=(0, 1, 2))
    for iteration in range(ITERS):
        scaled = lax.optimization_barrier((prior_scale * direction).astype(jnp.bfloat16))
        image = forward_map(footprints, block_sounding, block_tile, block_count, scaled)
        weighted = lax.optimization_barrier((weight * image).astype(jnp.bfloat16))
        product = direction + prior_scale * transpose_map(footprints, block_sounding, block_tile, block_count, weighted)
        step_size = norm_now / jnp.sum(direction * product, axis=(0, 1, 2))
        iterate = iterate + step_size * direction
        residual = residual - step_size * product
        if iteration + 1 < ITERS:
            norm_next = jnp.sum(residual * residual, axis=(0, 1, 2))
            direction = residual + (norm_next / norm_now) * direction
            norm_now = norm_next
    return prior_scale * iterate, residual
```

```python
import functools

import jax
import jax.numpy as jnp
from jax import lax
from jax.experimental import pallas as pl
from jax.experimental.pallas import tpu as pltpu
from jax.sharding import PartitionSpec as P

F32 = jnp.float32
BF16 = jnp.bfloat16
I16 = jnp.int16
GROUP = 4
EXTRA = 16
FULL = 32000.0
VMEM_LIMIT = 24 * 1024 * 1024


def partner(index, step, count):
    if count & (count - 1) == 0:
        return index ^ step
    return (index + step) % count if isinstance(index, int) else lax.rem(index + step, count)


def sender(index, step, count):
    if count & (count - 1) == 0:
        return index ^ step
    return lax.rem(index + count - step, count)


def rows_of(rows):
    width = rows[0].shape[1]
    which = lax.broadcasted_iota(jnp.int32, (EXTRA, width), 0)
    out = jnp.zeros((EXTRA, width), F32)
    for k, row in enumerate(rows):
        out = jnp.where(which == k, row, out)
    return out


def exponent_of(row):
    return jnp.floor(jnp.log2(jnp.maximum(row, 1e-30))) + 1.0


def put_coded(ref, value, sums):
    size = value.shape[0]
    exponent = exponent_of(jnp.max(jnp.abs(value), axis=0, keepdims=True))
    scale = jnp.exp2(15.0 - exponent) * (FULL / 32768.0)
    ref[0:size, :] = jnp.round(value * scale).astype(jnp.int32).astype(I16)
    rows = [exponent]
    for row in sums:
        power = exponent_of(jnp.abs(row))
        number = row * (jnp.exp2(15.0 - power) * (FULL / 32768.0))
        head = jnp.round(number)
        rows += [power, head, jnp.round((number - head) * FULL)]
    ref[size : size + EXTRA, :] = rows_of(rows).astype(jnp.int32).astype(I16)


def get_coded(ref, size, n_sums):
    extra = ref[size : size + EXTRA, :].astype(jnp.int32).astype(F32)
    scale = jnp.exp2(extra[0:1] - 15.0) * (32768.0 / FULL)
    value = ref[0:size, :].astype(jnp.int32).astype(F32) * scale
    sums = []
    for k in range(n_sums):
        base = 1 + 3 * k
        number = extra[base + 1 : base + 2] + extra[base + 2 : base + 3] * (1.0 / FULL)
        sums.append(number * (jnp.exp2(extra[base : base + 1] - 15.0) * (32768.0 / FULL)))
    return value, sums


def split_rows(sums):
    rows = []
    for row in sums:
        head = row.astype(BF16).astype(F32)
        middle = (row - head).astype(BF16).astype(F32)
        rows += [head, middle, row - head - middle]
    return rows_of(rows).astype(BF16)


def join_rows(extra, n_sums):
    extra = extra.astype(F32)
    return [
        extra[3 * k : 3 * k + 1] + extra[3 * k + 1 : 3 * k + 2] + extra[3 * k + 2 : 3 * k + 3]
        for k in range(n_sums)
    ]


def column_of(row):
    parts = []
    for k in range(row.shape[1] // 128):
        part = jnp.broadcast_to(row[:, 128 * k : 128 * k + 128], (128, 128))
        parts.append(jnp.transpose(part))
    return jnp.concatenate(parts, axis=0)


def place_pair(low_ref, high_ref, pair, value):
    lane = lax.broadcasted_iota(jnp.int32, value.shape, 1)
    half = value.shape[1] // 2
    low = lane < half
    turned = pltpu.roll(value, half, 1)
    zero = jnp.zeros_like(value)
    low_ref[2 * pair] = jnp.where(low, value, zero).astype(BF16)
    high_ref[2 * pair] = jnp.where(low, zero, turned).astype(BF16)
    low_ref[2 * pair + 1] = jnp.where(low, turned, zero).astype(BF16)
    high_ref[2 * pair + 1] = jnp.where(low, zero, value).astype(BF16)


def transpose_tiles(plan, lists, orbit, n_orbit, footprints, low_ref, high_ref, emit):
    cells = footprints.shape[2]
    members = low_ref.shape[1]
    n_blocks = (lists - n_orbit - 1) // 2

    for step in range(n_orbit):
        tile = partner(orbit, step, n_orbit)

        def turn(group, total):
            spots = [GROUP * group + k for k in range(GROUP)]
            blocks = [plan[spot] for spot in spots]
            sounds = [plan[n_blocks + spot] for spot in spots]
            left = jnp.concatenate(
                [
                    low_ref[sounds[k]] + high_ref[sounds[k + 1]]
                    for k in range(0, GROUP, 2)
                ],
                axis=1,
            )
            right = jnp.concatenate([footprints[block] for block in blocks], axis=0)
            return total + jnp.dot(left, right, preferred_element_type=F32)

        begin = plan[2 * n_blocks + tile]
        end = plan[2 * n_blocks + tile + 1]
        total = lax.fori_loop(begin, end, turn, jnp.zeros((members, cells), F32))
        emit(step, jnp.transpose(total))


def forward_tiles(plan, lists, orbit, n_orbit, footprints, fields, total_ref):
    n_blocks = (lists - n_orbit - 1) // 2
    depth = footprints.shape[1]
    total_ref[...] = jnp.zeros_like(total_ref)
    for step in range(n_orbit):
        tile = sender(orbit, step, n_orbit)
        field = fields(step)

        def turn(group, carry):
            spots = [GROUP * group + k for k in range(GROUP)]
            left = jnp.concatenate([footprints[plan[spot]] for spot in spots], axis=0)
            product = jnp.dot(left, field, preferred_element_type=F32)
            for k, spot in enumerate(spots):
                sound = plan[n_blocks + spot]
                total_ref[sound] = total_ref[sound] + product[depth * k : depth * k + depth]
            return carry

        lax.fori_loop(plan[2 * n_blocks + tile], plan[2 * n_blocks + tile + 1], turn, 0)


def first_kernel(
    n_orbit, lists, place, sounding, tile_of, count, footprints_hbm, observed, weight, *rest
):
    outs, (footprints, plan, low_ref, high_ref, counter, copy_sem) = (
        rest[:n_orbit],
        rest[n_orbit:],
    )
    copy = pltpu.make_async_copy(footprints_hbm, footprints, copy_sem)
    copy.start()
    n_blocks = (lists - n_orbit - 1) // 2
    sb_count = observed.shape[0]
    live = count[0]

    def clear(tile, carry):
        counter[tile] = 0
        return carry

    lax.fori_loop(0, n_orbit, clear, 0)

    def tally(spot, carry):
        tile = tile_of[spot]
        counter[tile] = counter[tile] + 1
        return carry

    lax.fori_loop(0, live, tally, 0)

    def begin(tile, group):
        plan[2 * n_blocks + tile] = group
        after = group + (counter[tile] + (GROUP - 1)) // GROUP
        counter[tile] = group * GROUP
        return after

    plan[2 * n_blocks + n_orbit] = lax.fori_loop(0, n_orbit, begin, 0)

    def sort(spot, carry):
        tile = tile_of[spot]
        slot = counter[tile]
        counter[tile] = slot + 1
        plan[slot] = spot
        plan[n_blocks + slot] = sounding[spot]
        return carry

    lax.fori_loop(0, live, sort, 0)

    def fill(tile, carry):
        def blank(slot, inner):
            plan[slot] = 0
            plan[n_blocks + slot] = sb_count
            return inner

        end = plan[2 * n_blocks + tile + 1] * GROUP
        lax.fori_loop(counter[tile], end, blank, 0)
        return carry

    lax.fori_loop(0, n_orbit, fill, 0)

    low_ref[sb_count] = jnp.zeros(low_ref.shape[1:], BF16)
    high_ref[sb_count] = jnp.zeros(high_ref.shape[1:], BF16)
    for pair in range(sb_count // 2):
        both = jnp.concatenate([observed[2 * pair], observed[2 * pair + 1]], axis=0)
        value = (jnp.transpose(both) * weight[pair : pair + 1, :]).astype(BF16).astype(F32)
        place_pair(low_ref, high_ref, pair, value)
    copy.wait()

    def emit(step, value):
        if step == 0:
            outs[0][...] = value
        else:
            put_coded(outs[step], value, [])

    transpose_tiles(plan, lists, place[0], n_orbit, footprints, low_ref, high_ref, emit)


def transpose_kernel(n_orbit, n_region, lists, place, plan, footprints, *rest):
    parts = rest[:n_region]
    outs = rest[n_region : n_region + n_orbit]
    own_sum, low_ref, high_ref = rest[n_region + n_orbit :]
    share = parts[0].shape[0] - EXTRA
    pairs = share // 128
    sb_count = low_ref.shape[0] - 1
    low_ref[sb_count] = jnp.zeros(low_ref.shape[1:], BF16)
    high_ref[sb_count] = jnp.zeros(high_ref.shape[1:], BF16)
    dot = jnp.zeros((1, parts[0].shape[1]), F32)
    for step in range(n_region):
        owner = sender(place[1], step, n_region)
        for pair in range(pairs):
            value = parts[step][128 * pair : 128 * pair + 128, :].astype(F32)
            place_pair(low_ref, high_ref, owner * pairs + pair, value)
        dot = dot + join_rows(parts[step][share : share + EXTRA, :], 1)[0]
    own_sum[...] = jnp.broadcast_to(dot, own_sum.shape)

    def emit(step, value):
        if step == 0:
            outs[0][...] = value
        else:
            put_coded(outs[step], value, [dot])

    transpose_tiles(plan, lists, place[0], n_orbit, footprints, low_ref, high_ref, emit)


def forward_kernel(n_orbit, n_region, n_sums, lists, place, plan, footprints, *rest):
    parts = rest[:n_orbit]
    outs = rest[n_orbit : n_orbit + n_region]
    own_sums, total_ref = rest[n_orbit + n_region :]
    cells = footprints.shape[2]
    depth = footprints.shape[1]
    sb_count = total_ref.shape[0] - 1
    members = total_ref.shape[2]
    share = sb_count // n_region

    sums = [jnp.zeros((1, members), F32) for _ in range(n_sums)]
    for step in range(n_orbit):
        got = join_rows(parts[step][cells : cells + EXTRA, :], n_sums)
        sums = [a + b for a, b in zip(sums, got)]
    own_sums[...] = rows_of(sums)[0:8]
    forward_tiles(
        plan, lists, place[0], n_orbit, footprints, lambda step: parts[step][0:cells, :], total_ref
    )
    for step in range(n_region):
        owner = partner(place[1], step, n_region)
        value = total_ref[pl.ds(owner * share, share)].reshape(share * depth, members)
        if step == 0:
            outs[0][...] = value
        else:
            put_coded(outs[step], value, sums)


def field_kernel(n_orbit, prior, *rest):
    parts = rest[:n_orbit]
    right_ref, send_ref = rest[n_orbit:]
    cells = parts[0].shape[0]
    total = parts[0][...]
    for step in range(1, n_orbit):
        total = total + get_coded(parts[step], cells, 0)[0]
    scale = column_of(prior[...])
    right = scale * total
    right_ref[...] = right
    send_ref[0:cells, :] = (scale * right).astype(BF16)
    send_ref[cells : cells + EXTRA, :] = split_rows([jnp.sum(right * right, axis=0, keepdims=True)])


def weigh_kernel(n_region, second, weight, own_sums, *rest):
    parts = rest[:n_region]
    rest = rest[n_region:]
    n_sums = 2 if second else 1
    size = parts[0].shape[0]
    image = parts[0][...]
    sums = [own_sums[k : k + 1, :] for k in range(n_sums)]
    for step in range(1, n_region):
        value, got = get_coded(parts[step], size, n_sums)
        image = image + value
        sums = [a + b for a, b in zip(sums, got)]
    if second:
        first_image, first_norm, send_ref, norm_ref = rest
        norm_old = first_norm[0:1, :]
        norm_new, cross = sums
        beta = norm_new / norm_old
        image = image + beta * first_image[...]
        length = norm_new + 2.0 * beta * cross + beta * beta * norm_old
        norm_ref[...] = rows_of([norm_new, beta, length])[0:8]
    else:
        send_ref, image_ref, norm_ref = rest
        image_ref[...] = image
        norm_ref[...] = rows_of(sums)[0:8]
    dot = jnp.zeros((1, image.shape[1]), F32)
    for pair in range(size // 128):
        piece = image[128 * pair : 128 * pair + 128]
        weighted = (column_of(weight[pair : pair + 1, :]) * piece).astype(BF16).astype(F32)
        dot = dot + jnp.sum(piece * weighted, axis=0, keepdims=True)
        send_ref[128 * pair : 128 * pair + 128, :] = jnp.transpose(weighted).astype(BF16)
    send_ref[size : size + EXTRA, :] = split_rows([dot])


def middle_kernel(n_orbit, prior, own_sum, norm, right_ref, *rest):
    parts = rest[:n_orbit]
    residual_ref, iterate_ref, send_ref = rest[n_orbit:]
    cells = parts[0].shape[0]
    total = parts[0][...]
    dot = own_sum[0:1, :]
    for step in range(1, n_orbit):
        value, got = get_coded(parts[step], cells, 1)
        total = total + value
        dot = dot + got[0]
    scale = column_of(prior[...])
    right = right_ref[...]
    norm_now = norm[0:1, :]
    step_size = norm_now / (norm_now + dot)
    product = right + scale * total
    residual = right - step_size * product
    residual_ref[...] = residual
    iterate_ref[...] = step_size * right
    send_ref[0:cells, :] = (scale * residual).astype(BF16)
    send_ref[cells : cells + EXTRA, :] = split_rows(
        [
            jnp.sum(residual * residual, axis=0, keepdims=True),
            jnp.sum(residual * right, axis=0, keepdims=True),
        ]
    )


def last_kernel(n_orbit, prior, own_sum, norm, right_ref, residual_ref, iterate_ref, *rest):
    parts = rest[:n_orbit]
    flux_out, residual_out = rest[n_orbit:]
    cells = parts[0].shape[0]
    total = parts[0][...]
    dot = own_sum[0:1, :]
    for step in range(1, n_orbit):
        value, got = get_coded(parts[step], cells, 1)
        total = total + value
        dot = dot + got[0]
    scale = column_of(prior[...])
    norm_now, beta, length = norm[0:1, :], norm[1:2, :], norm[2:3, :]
    residual = residual_ref[...]
    direction = residual + beta * right_ref[...]
    product = direction + scale * total
    step_size = norm_now / (length + dot)
    flux_out[...] = scale * (iterate_ref[...] + step_size * direction)
    residual_out[...] = residual - step_size * product


def per_device(
    n_orbit, n_region, footprints, sounding, tile_of, count, observations, obs_weight, prior_std
):
    n_slots, depth, cells = footprints.shape
    sb_count, _, members = observations.shape
    n_blocks = (n_slots + n_orbit * (GROUP - 1) + GROUP - 1) // GROUP * GROUP
    lists = 2 * n_blocks + n_orbit + 1
    share = sb_count // n_region
    size = share * depth
    orbit, region = lax.axis_index("orbit"), lax.axis_index("region")
    place = jnp.stack([orbit, region]).astype(jnp.int32)
    prior = prior_std.reshape(1, cells)
    weight = obs_weight.reshape(sb_count * depth // 128, 128)
    own_weight = lax.dynamic_slice_in_dim(weight, region * (size // 128), size // 128, 0)

    smem = pl.BlockSpec(memory_space=pltpu.SMEM)
    vmem = pl.BlockSpec(memory_space=pltpu.VMEM)
    params = pltpu.CompilerParams(vmem_limit_bytes=VMEM_LIMIT)

    def shape(*dims, dtype=F32):
        return jax.ShapeDtypeStruct(dims, dtype)

    def call(kernel, ins, outs, scratch=()):
        specs = [spec for spec, _ in ins]
        return pl.pallas_call(
            kernel,
            in_specs=specs,
            out_specs=[spec for spec, _ in outs],
            out_shape=[s for _, s in outs],
            scratch_shapes=list(scratch),
            compiler_params=params,
        )(*[value for _, value in ins])

    def exchange(values, axis, total):
        got = [values[0]]
        for step in range(1, total):
            pairs = [(i, partner(i, step, total)) for i in range(total)]
            got.append(lax.ppermute(values[step], axis, pairs))
        return got

    def spread(value, axis, total):
        return exchange([value] * total, axis, total)

    low_high = [
        pltpu.VMEM((sb_count + 1, members, 2 * depth), BF16),
        pltpu.VMEM((sb_count + 1, members, 2 * depth), BF16),
    ]
    tile_outs = [(vmem, shape(cells, members))] + [
        (vmem, shape(cells + EXTRA, members, dtype=I16)) for _ in range(n_orbit - 1)
    ]
    row_out = (vmem, shape(8, members))
    field_out = (vmem, shape(cells, members))
    send_out = (vmem, shape(cells + EXTRA, members, dtype=BF16))

    *tiles, held, plan = call(
        functools.partial(first_kernel, n_orbit, lists),
        [
            (smem, place),
            (smem, sounding),
            (smem, tile_of),
            (smem, count),
            (pl.BlockSpec(memory_space=pl.ANY), footprints),
            (vmem, observations),
            (vmem, weight),
        ],
        tile_outs
        + [
            (vmem, pltpu.VMEM(footprints.shape, BF16)),
            (smem, shape(lists, dtype=jnp.int32)),
        ],
        low_high + [pltpu.SMEM((n_orbit,), jnp.int32), pltpu.SemaphoreType.DMA],
    )
    held = pltpu.with_memory_space_constraint(held, pltpu.VMEM)

    def forward(parts, n_sums):
        outs = call(
            functools.partial(forward_kernel, n_orbit, n_region, n_sums, lists),
            [(smem, place), (smem, plan), (vmem, held)] + [(vmem, part) for part in parts],
            [(vmem, shape(size, members))]
            + [(vmem, shape(size + EXTRA, members, dtype=I16)) for _ in range(n_region - 1)]
            + [row_out],
            [pltpu.VMEM((sb_count + 1, depth, members), F32)],
        )
        return exchange(outs[:n_region], "region", n_region), outs[n_region]

    def transpose(parts):
        outs = call(
            functools.partial(transpose_kernel, n_orbit, n_region, lists),
            [(smem, place), (smem, plan), (vmem, held)] + [(vmem, part) for part in parts],
            tile_outs + [row_out],
            low_high,
        )
        return exchange(outs[:n_orbit], "orbit", n_orbit), outs[n_orbit]

    weighted_out = (vmem, shape(size + EXTRA, members, dtype=BF16))

    tiles = exchange(tiles, "orbit", n_orbit)
    right, send = call(
        functools.partial(field_kernel, n_orbit),
        [(vmem, prior)] + [(vmem, tile) for tile in tiles],
        [field_out, send_out],
    )

    parts, sums = forward(spread(send, "orbit", n_orbit), 1)
    send, image, norm = call(
        functools.partial(weigh_kernel, n_region, False),
        [(vmem, own_weight), (vmem, sums)] + [(vmem, part) for part in parts],
        [weighted_out, (vmem, shape(size, members)), row_out],
    )
    tiles, own_sum = transpose(spread(send, "region", n_region))
    residual, iterate, send = call(
        functools.partial(middle_kernel, n_orbit),
        [(vmem, prior), (vmem, own_sum), (vmem, norm), (vmem, right)]
        + [(vmem, tile) for tile in tiles],
        [field_out, field_out, send_out],
    )

    parts, sums = forward(spread(send, "orbit", n_orbit), 2)
    send, norms = call(
        functools.partial(weigh_kernel, n_region, True),
        [(vmem, own_weight), (vmem, sums)]
        + [(vmem, part) for part in parts]
        + [(vmem, image), (vmem, norm)],
        [weighted_out, row_out],
    )
    tiles, own_sum = transpose(spread(send, "region", n_region))
    flux, residual = call(
        functools.partial(last_kernel, n_orbit),
        [(vmem, prior), (vmem, own_sum), (vmem, norms)]
        + [(vmem, right), (vmem, residual), (vmem, iterate)]
        + [(vmem, tile) for tile in tiles],
        [field_out, field_out],
    )
    return flux[None, None], residual[None, None]


def solution(mesh):
    n_orbit, n_region = mesh.shape["orbit"], mesh.shape["region"]
    return jax.shard_map(
        functools.partial(per_device, n_orbit, n_region),
        mesh=mesh,
        in_specs=(
            P(("orbit", "region"), None, None),
            P(("orbit", "region")),
            P(("orbit", "region")),
            P(("orbit", "region")),
            P("orbit", None, None),
            P("orbit", None),
            P("region", "orbit", None),
        ),
        out_specs=(P("region", "orbit", None, None), P("region", "orbit", None, None)),
        check_vma=False,
    )
```

```python
import functools

import jax
import jax.numpy as jnp
from jax import lax
from jax.experimental import pallas as pl
from jax.experimental.pallas import tpu as pltpu
from jax.sharding import PartitionSpec as P

F32 = jnp.float32
BF16 = jnp.bfloat16
I16 = jnp.int16
GROUP = 4
TURN = 8
EXTRA = 16
FULL = 32000.0
VMEM_LIMIT = 24 * 1024 * 1024


def partner(index, step, count):
    if count & (count - 1) == 0:
        return index ^ step
    return (index + step) % count if isinstance(index, int) else lax.rem(index + step, count)


def slot_of(tile, index, count):
    if count & (count - 1) == 0:
        return tile ^ index
    return lax.rem(tile + count - index, count)


def rows_of(rows):
    width = rows[0].shape[1]
    which = lax.broadcasted_iota(jnp.int32, (EXTRA, width), 0)
    out = jnp.zeros((EXTRA, width), F32)
    for k, row in enumerate(rows):
        out = jnp.where(which == k, row, out)
    return out


def exponent_of(row):
    return jnp.floor(jnp.log2(jnp.maximum(row, 1e-30))) + 1.0


def put_coded(ref, value, sums):
    size = value.shape[0]
    exponent = exponent_of(jnp.max(jnp.abs(value), axis=0, keepdims=True))
    scale = jnp.exp2(15.0 - exponent) * (FULL / 32768.0)
    ref[0:size, :] = jnp.round(value * scale).astype(jnp.int32).astype(I16)
    rows = [exponent]
    for row in sums:
        power = exponent_of(jnp.abs(row))
        number = row * (jnp.exp2(15.0 - power) * (FULL / 32768.0))
        head = jnp.round(number)
        rows += [power, head, jnp.round((number - head) * FULL)]
    ref[size : size + EXTRA, :] = rows_of(rows).astype(jnp.int32).astype(I16)


def get_coded(ref, size, n_sums):
    extra = ref[size : size + EXTRA, :].astype(jnp.int32).astype(F32)
    scale = jnp.exp2(extra[0:1] - 15.0) * (32768.0 / FULL)
    value = ref[0:size, :].astype(jnp.int32).astype(F32) * scale
    sums = []
    for k in range(n_sums):
        base = 1 + 3 * k
        number = extra[base + 1 : base + 2] + extra[base + 2 : base + 3] * (1.0 / FULL)
        sums.append(number * (jnp.exp2(extra[base : base + 1] - 15.0) * (32768.0 / FULL)))
    return value, sums


def split_rows(sums):
    rows = []
    for row in sums:
        head = row.astype(BF16).astype(F32)
        middle = (row - head).astype(BF16).astype(F32)
        rows += [head, middle, row - head - middle]
    return rows_of(rows).astype(BF16)


def join_rows(extra, n_sums):
    extra = extra.astype(F32)
    return [
        extra[3 * k : 3 * k + 1] + extra[3 * k + 1 : 3 * k + 2] + extra[3 * k + 2 : 3 * k + 3]
        for k in range(n_sums)
    ]


def column_of(row):
    parts = []
    for k in range(row.shape[1] // 128):
        part = jnp.broadcast_to(row[:, 128 * k : 128 * k + 128], (128, 128))
        parts.append(jnp.transpose(part))
    return jnp.concatenate(parts, axis=0)


def place_pair(low_ref, high_ref, pair, value):
    lane = lax.broadcasted_iota(jnp.int32, value.shape, 1)
    half = value.shape[1] // 2
    low = lane < half
    turned = pltpu.roll(value, half, 1)
    zero = jnp.zeros_like(value)
    low_ref[2 * pair] = jnp.where(low, value, zero).astype(BF16)
    high_ref[2 * pair] = jnp.where(low, zero, turned).astype(BF16)
    low_ref[2 * pair + 1] = jnp.where(low, turned, zero).astype(BF16)
    high_ref[2 * pair + 1] = jnp.where(low, zero, value).astype(BF16)


class Lists:
    def __init__(self, n_slots, n_tiles):
        groups = (n_slots + GROUP - 1) // GROUP + n_tiles
        self.groups = (groups + TURN - 1) // TURN * TURN
        self.sounds = self.groups * GROUP
        self.tiles = 2 * self.sounds
        self.turns = self.tiles + self.groups
        self.size = self.turns + 1


def transpose_tiles(plan, lists, footprints, low_ref, high_ref, total_ref):
    total_ref[...] = jnp.zeros_like(total_ref)

    def turn(index, carry):
        products = []
        for group in range(TURN):
            spots = [GROUP * (index * TURN + group) + k for k in range(GROUP)]
            sounds = [plan[lists.sounds + spot] for spot in spots]
            left = jnp.concatenate(
                [
                    low_ref[sounds[k]] + high_ref[sounds[k + 1]]
                    for k in range(0, GROUP, 2)
                ],
                axis=1,
            )
            right = jnp.concatenate([footprints[plan[spot]] for spot in spots], axis=0)
            products.append(jnp.dot(left, right, preferred_element_type=F32))
        for group, product in enumerate(products):
            slot = plan[lists.tiles + index * TURN + group]
            total_ref[slot] = total_ref[slot] + product
        return carry

    lax.fori_loop(0, plan[lists.turns], turn, 0)


def forward_tiles(plan, lists, footprints, field_ref, total_ref):
    depth = footprints.shape[1]
    total_ref[...] = jnp.zeros_like(total_ref)

    def turn(index, carry):
        products = []
        for group in range(TURN):
            spots = [GROUP * (index * TURN + group) + k for k in range(GROUP)]
            left = jnp.concatenate([footprints[plan[spot]] for spot in spots], axis=0)
            slot = plan[lists.tiles + index * TURN + group]
            products.append(jnp.dot(left, field_ref[slot], preferred_element_type=F32))
        for group, product in enumerate(products):
            for k in range(GROUP):
                sound = plan[lists.sounds + GROUP * (index * TURN + group) + k]
                total_ref[sound] = total_ref[sound] + product[depth * k : depth * k + depth]
        return carry

    lax.fori_loop(0, plan[lists.turns], turn, 0)


def sort_blocks(plan, lists, orbit, n_orbit, sounding, tile_of, live, counter, sb_count):
    def clear(slot, carry):
        counter[slot] = 0
        return carry

    lax.fori_loop(0, n_orbit, clear, 0)

    def tally(block, carry):
        slot = slot_of(tile_of[block], orbit, n_orbit)
        counter[slot] = counter[slot] + 1
        return carry

    lax.fori_loop(0, live, tally, 0)

    def begin(slot, group):
        after = group + (counter[slot] + (GROUP - 1)) // GROUP
        counter[slot] = group * GROUP

        def name(index, carry):
            plan[lists.tiles + index] = slot
            return carry

        lax.fori_loop(group, after, name, 0)
        return after

    groups = lax.fori_loop(0, n_orbit, begin, 0)
    turns = (groups + (TURN - 1)) // TURN
    plan[lists.turns] = turns

    def rest(index, carry):
        plan[lists.tiles + index] = 0
        return carry

    lax.fori_loop(groups, turns * TURN, rest, 0)

    def blank(spot, carry):
        plan[spot] = 0
        plan[lists.sounds + spot] = sb_count
        return carry

    lax.fori_loop(0, turns * (TURN * GROUP), blank, 0)

    def sort(block, carry):
        slot = slot_of(tile_of[block], orbit, n_orbit)
        spot = counter[slot]
        counter[slot] = spot + 1
        plan[spot] = block
        plan[lists.sounds + spot] = sounding[block]
        return carry

    lax.fori_loop(0, live, sort, 0)


def put_tiles(outs, total_ref, sums):
    for step, out in enumerate(outs):
        value = jnp.transpose(total_ref[step])
        if step == 0:
            out[...] = value
        else:
            put_coded(out, value, sums)


def first_kernel(
    n_orbit, lists, place, sounding, tile_of, count, footprints_hbm, observed, weight, *rest
):
    outs = rest[:n_orbit]
    footprints, plan, low_ref, high_ref, total_ref, counter, copy_sem = rest[n_orbit:]
    copy = pltpu.make_async_copy(footprints_hbm, footprints, copy_sem)
    copy.start()
    sb_count = observed.shape[0]
    sort_blocks(
        plan, lists, place[0], n_orbit, sounding, tile_of, count[0], counter, sb_count
    )
    low_ref[sb_count] = jnp.zeros(low_ref.shape[1:], BF16)
    high_ref[sb_count] = jnp.zeros(high_ref.shape[1:], BF16)
    for pair in range(sb_count // 2):
        both = jnp.concatenate([observed[2 * pair], observed[2 * pair + 1]], axis=0)
        value = (jnp.transpose(both) * weight[pair : pair + 1, :]).astype(BF16).astype(F32)
        place_pair(low_ref, high_ref, pair, value)
    copy.wait()
    transpose_tiles(plan, lists, footprints, low_ref, high_ref, total_ref)
    put_tiles(outs, total_ref, [])


def transpose_kernel(n_orbit, n_region, lists, place, plan, footprints, *rest):
    parts = rest[:n_region]
    outs = rest[n_region : n_region + n_orbit]
    own_sum, held, low_ref, high_ref, total_ref = rest[n_region + n_orbit :]
    del held
    share = parts[0].shape[0] - EXTRA
    pairs = share // 128
    sb_count = low_ref.shape[0] - 1
    low_ref[sb_count] = jnp.zeros(low_ref.shape[1:], BF16)
    high_ref[sb_count] = jnp.zeros(high_ref.shape[1:], BF16)
    dot = jnp.zeros((1, parts[0].shape[1]), F32)
    for step in range(n_region):
        owner = partner(place[1], step, n_region)
        for pair in range(pairs):
            value = parts[step][128 * pair : 128 * pair + 128, :].astype(F32)
            place_pair(low_ref, high_ref, owner * pairs + pair, value)
        dot = dot + join_rows(parts[step][share : share + EXTRA, :], 1)[0]
    own_sum[...] = jnp.broadcast_to(dot, own_sum.shape)
    transpose_tiles(plan, lists, footprints, low_ref, high_ref, total_ref)
    put_tiles(outs, total_ref, [dot])


def forward_kernel(n_orbit, n_region, n_sums, lists, place, plan, footprints, *rest):
    parts = rest[:n_orbit]
    outs = rest[n_orbit : n_orbit + n_region]
    own_sums, held, field_ref, total_ref = rest[n_orbit + n_region :]
    del held
    cells = footprints.shape[2]
    depth = footprints.shape[1]
    sb_count = total_ref.shape[0] - 1
    members = total_ref.shape[2]
    share = sb_count // n_region

    sums = [jnp.zeros((1, members), F32) for _ in range(n_sums)]
    for step in range(n_orbit):
        got = join_rows(parts[step][cells : cells + EXTRA, :], n_sums)
        sums = [a + b for a, b in zip(sums, got)]
        field_ref[step] = parts[step][0:cells, :]
    own_sums[...] = rows_of(sums)[0:8]
    forward_tiles(plan, lists, footprints, field_ref, total_ref)
    for step in range(n_region):
        owner = partner(place[1], step, n_region)
        value = total_ref[pl.ds(owner * share, share)].reshape(share * depth, members)
        if step == 0:
            outs[0][...] = value
        else:
            put_coded(outs[step], value, sums)


def field_kernel(n_orbit, prior, *rest):
    parts = rest[:n_orbit]
    right_ref, send_ref = rest[n_orbit:]
    cells = parts[0].shape[0]
    total = parts[0][...]
    for step in range(1, n_orbit):
        total = total + get_coded(parts[step], cells, 0)[0]
    scale = column_of(prior[...])
    right = scale * total
    right_ref[...] = right
    send_ref[0:cells, :] = (scale * right).astype(BF16)
    send_ref[cells : cells + EXTRA, :] = split_rows([jnp.sum(right * right, axis=0, keepdims=True)])


def weigh_kernel(n_region, second, weight, own_sums, *rest):
    parts = rest[:n_region]
    rest = rest[n_region:]
    n_sums = 2 if second else 1
    size = parts[0].shape[0]
    image = parts[0][...]
    sums = [own_sums[k : k + 1, :] for k in range(n_sums)]
    for step in range(1, n_region):
        value, got = get_coded(parts[step], size, n_sums)
        image = image + value
        sums = [a + b for a, b in zip(sums, got)]
    if second:
        first_image, first_norm, send_ref, norm_ref = rest
        norm_old = first_norm[0:1, :]
        norm_new, cross = sums
        beta = norm_new / norm_old
        image = image + beta * first_image[...]
        length = norm_new + 2.0 * beta * cross + beta * beta * norm_old
        norm_ref[...] = rows_of([norm_new, beta, length])[0:8]
    else:
        send_ref, image_ref, norm_ref = rest
        image_ref[...] = image
        norm_ref[...] = rows_of(sums)[0:8]
    dot = jnp.zeros((1, image.shape[1]), F32)
    for pair in range(size // 128):
        piece = image[128 * pair : 128 * pair + 128]
        weighted = (column_of(weight[pair : pair + 1, :]) * piece).astype(BF16).astype(F32)
        dot = dot + jnp.sum(piece * weighted, axis=0, keepdims=True)
        send_ref[128 * pair : 128 * pair + 128, :] = jnp.transpose(weighted).astype(BF16)
    send_ref[size : size + EXTRA, :] = split_rows([dot])


def middle_kernel(n_orbit, prior, own_sum, norm, right_ref, *rest):
    parts = rest[:n_orbit]
    residual_ref, iterate_ref, send_ref = rest[n_orbit:]
    cells = parts[0].shape[0]
    total = parts[0][...]
    dot = own_sum[0:1, :]
    for step in range(1, n_orbit):
        value, got = get_coded(parts[step], cells, 1)
        total = total + value
        dot = dot + got[0]
    scale = column_of(prior[...])
    right = right_ref[...]
    norm_now = norm[0:1, :]
    step_size = norm_now / (norm_now + dot)
    product = right + scale * total
    residual = right - step_size * product
    residual_ref[...] = residual
    iterate_ref[...] = step_size * right
    send_ref[0:cells, :] = (scale * residual).astype(BF16)
    send_ref[cells : cells + EXTRA, :] = split_rows(
        [
            jnp.sum(residual * residual, axis=0, keepdims=True),
            jnp.sum(residual * right, axis=0, keepdims=True),
        ]
    )


def last_kernel(n_orbit, prior, own_sum, norm, right_ref, residual_ref, iterate_ref, *rest):
    parts = rest[:n_orbit]
    flux_out, residual_out = rest[n_orbit:]
    cells = parts[0].shape[0]
    total = parts[0][...]
    dot = own_sum[0:1, :]
    for step in range(1, n_orbit):
        value, got = get_coded(parts[step], cells, 1)
        total = total + value
        dot = dot + got[0]
    scale = column_of(prior[...])
    norm_now, beta, length = norm[0:1, :], norm[1:2, :], norm[2:3, :]
    residual = residual_ref[...]
    direction = residual + beta * right_ref[...]
    product = direction + scale * total
    step_size = norm_now / (length + dot)
    flux_out[...] = scale * (iterate_ref[...] + step_size * direction)
    residual_out[...] = residual - step_size * product


def per_device(
    n_orbit, n_region, footprints, sounding, tile_of, count, observations, obs_weight, prior_std
):
    n_slots, depth, cells = footprints.shape
    sb_count, _, members = observations.shape
    lists = Lists(n_slots, n_orbit)
    share = sb_count // n_region
    size = share * depth
    orbit, region = lax.axis_index("orbit"), lax.axis_index("region")
    place = jnp.stack([orbit, region]).astype(jnp.int32)
    prior = prior_std.reshape(1, cells)
    weight = obs_weight.reshape(sb_count * depth // 128, 128)
    own_weight = lax.dynamic_slice_in_dim(weight, region * (size // 128), size // 128, 0)

    smem = pl.BlockSpec(memory_space=pltpu.SMEM)
    vmem = pl.BlockSpec(memory_space=pltpu.VMEM)
    params = pltpu.CompilerParams(vmem_limit_bytes=VMEM_LIMIT)

    def shape(*dims, dtype=F32):
        return jax.ShapeDtypeStruct(dims, dtype)

    def call(kernel, ins, outs, scratch=(), alias=()):
        specs = [spec for spec, _ in ins]
        return pl.pallas_call(
            kernel,
            in_specs=specs,
            out_specs=[spec for spec, _ in outs],
            out_shape=[s for _, s in outs],
            scratch_shapes=list(scratch),
            input_output_aliases=dict(alias),
            compiler_params=params,
        )(*[value for _, value in ins])

    def exchange(values, axis, total):
        got = [values[0]]
        for step in range(1, total):
            pairs = [(i, partner(i, step, total)) for i in range(total)]
            got.append(lax.ppermute(values[step], axis, pairs))
        return got

    def spread(value, axis, total):
        got = [value]
        for step in range(1, total):
            pairs = [(partner(i, step, total), i) for i in range(total)]
            got.append(lax.ppermute(value, axis, pairs))
        return got

    low_high = [
        pltpu.VMEM((sb_count + 1, members, 2 * depth), BF16),
        pltpu.VMEM((sb_count + 1, members, 2 * depth), BF16),
        pltpu.VMEM((n_orbit, members, cells), F32),
    ]
    held_out = (vmem, pltpu.VMEM(footprints.shape, BF16))
    tile_outs = [(vmem, shape(cells, members))] + [
        (vmem, shape(cells + EXTRA, members, dtype=I16)) for _ in range(n_orbit - 1)
    ]
    row_out = (vmem, shape(8, members))
    field_out = (vmem, shape(cells, members))
    send_out = (vmem, shape(cells + EXTRA, members, dtype=BF16))

    *tiles, held, plan = call(
        functools.partial(first_kernel, n_orbit, lists),
        [
            (smem, place),
            (smem, sounding),
            (smem, tile_of),
            (smem, count),
            (
                pl.BlockSpec(memory_space=pltpu.HBM),
                pltpu.with_memory_space_constraint(footprints, pltpu.HBM),
            ),
            (vmem, observations),
            (vmem, weight),
        ],
        tile_outs + [held_out, (smem, shape(lists.size, dtype=jnp.int32))],
        low_high + [pltpu.SMEM((n_orbit,), jnp.int32), pltpu.SemaphoreType.DMA],
    )

    def forward(held, parts, n_sums):
        *outs, sums, held = call(
            functools.partial(forward_kernel, n_orbit, n_region, n_sums, lists),
            [(smem, place), (smem, plan), (vmem, held)] + [(vmem, part) for part in parts],
            [(vmem, shape(size, members))]
            + [(vmem, shape(size + EXTRA, members, dtype=I16)) for _ in range(n_region - 1)]
            + [row_out, held_out],
            [
                pltpu.VMEM((n_orbit, cells, members), BF16),
                pltpu.VMEM((sb_count + 1, depth, members), F32),
            ],
            [(2, n_region + 1)],
        )
        return held, exchange(outs, "region", n_region), sums

    def transpose(held, parts):
        *outs, own_sum, held = call(
            functools.partial(transpose_kernel, n_orbit, n_region, lists),
            [(smem, place), (smem, plan), (vmem, held)] + [(vmem, part) for part in parts],
            tile_outs + [row_out, held_out],
            low_high,
            [(2, n_orbit + 1)],
        )
        return held, exchange(outs, "orbit", n_orbit), own_sum

    weighted_out = (vmem, shape(size + EXTRA, members, dtype=BF16))

    tiles = exchange(tiles, "orbit", n_orbit)
    right, send = call(
        functools.partial(field_kernel, n_orbit),
        [(vmem, prior)] + [(vmem, tile) for tile in tiles],
        [field_out, send_out],
    )

    held, parts, sums = forward(held, spread(send, "orbit", n_orbit), 1)
    send, image, norm = call(
        functools.partial(weigh_kernel, n_region, False),
        [(vmem, own_weight), (vmem, sums)] + [(vmem, part) for part in parts],
        [weighted_out, (vmem, shape(size, members)), row_out],
    )
    held, tiles, own_sum = transpose(held, spread(send, "region", n_region))
    residual, iterate, send = call(
        functools.partial(middle_kernel, n_orbit),
        [(vmem, prior), (vmem, own_sum), (vmem, norm), (vmem, right)]
        + [(vmem, tile) for tile in tiles],
        [field_out, field_out, send_out],
    )

    held, parts, sums = forward(held, spread(send, "orbit", n_orbit), 2)
    send, norms = call(
        functools.partial(weigh_kernel, n_region, True),
        [(vmem, own_weight), (vmem, sums)]
        + [(vmem, part) for part in parts]
        + [(vmem, image), (vmem, norm)],
        [weighted_out, row_out],
    )
    held, tiles, own_sum = transpose(held, spread(send, "region", n_region))
    flux, residual = call(
        functools.partial(last_kernel, n_orbit),
        [(vmem, prior), (vmem, own_sum), (vmem, norms)]
        + [(vmem, right), (vmem, residual), (vmem, iterate)]
        + [(vmem, tile) for tile in tiles],
        [field_out, field_out],
    )
    return flux[None, None], residual[None, None]


def solution(mesh):
    n_orbit, n_region = mesh.shape["orbit"], mesh.shape["region"]
    return jax.shard_map(
        functools.partial(per_device, n_orbit, n_region),
        mesh=mesh,
        in_specs=(
            P(("orbit", "region"), None, None),
            P(("orbit", "region")),
            P(("orbit", "region")),
            P(("orbit", "region")),
            P("orbit", None, None),
            P("orbit", None),
            P("region", "orbit", None),
        ),
        out_specs=(P("region", "orbit", None, None), P("region", "orbit", None, None)),
        check_vma=False,
    )
```
